512 devices in a mesh: row: 64 (over z, y), col: 8 (over x, core).
Axes of the slice: x: 4, y: 4, z: 16, core: 2. Of those that a mesh axis runs over, the one named last changes fastest.
Arguments:
- panel: float32 [65536, 512], P(('row', 'col')), may hold values from -1.2 to 1.2
- inverse_factor: float32 [512, 512], replicated, as said below
- slab: bfloat16 [65536, 8192], P('row', 'col'), may hold values from -6 to 6
Outputs:
- factor_panel: bfloat16 [65536, 512], P(('row', 'col'))
- updated_slab: bfloat16 [65536, 8192], P('row', 'col')
The draws below stay inside these ranges and needn't reach their ends.
Inputs may be any that keep to these rules, and one draw needn't show every extreme that they name: `inverse_factor`: lower triangular with a positive diagonal.
All inputs are finite; a program needn't handle non-finite values.
Results may differ from the reference program's by a relative error of at most 0.0052.
Values may be sent and summed in bfloat16 or wider, within the bound.
No kernel may reach another device: no remote copies, remote signals or barrier semaphores. Data moves between devices by JAX's collectives and lax.ppermute only.
A program may use at most 64 MiB of HBM per device.

```python
import math
import jax
import jax.numpy as jnp
from jax import lax

NB = 512
TILE = 128
M_DEV = 1024
ORDER = 65536
SLAB = 8192
SLAB_DEV = 1024
N_COL = 8


def draw_inverse_factor(key, part):
    key = jax.random.fold_in(key, 7)
    key_off, key_diag = jax.random.split(key)
    row_index = lax.broadcasted_iota(jnp.int32, (NB, NB), 0)
    col_index = lax.broadcasted_iota(jnp.int32, (NB, NB), 1)
    lower = jax.random.normal(key_off, (NB, NB), jnp.float32) * 0.5 * (1.0 / NB) ** 0.5
    diag_values = jnp.exp(jax.random.uniform(key_diag, (NB,), jnp.float32, math.log(0.5), math.log(2.0)))
    diag_full = jnp.broadcast_to(diag_values[:, None], (NB, NB))
    return jnp.where(row_index > col_index, lower, jnp.where(row_index == col_index, diag_full, 0.0)).astype(jnp.float32)


def block_levels(own_key, dims, pieces, smallest, top_value):
    loudness, own = 1.0, jax.random.fold_in(own_key, 6)
    for axis_at, parts in pieces:
        heights = jnp.exp(jax.random.uniform(jax.random.fold_in(own, axis_at), (parts,), jnp.float32, smallest / len(pieces), top_value / len(pieces)))
        loudness = loudness * jnp.repeat(heights, dims[axis_at] // parts).reshape([-1 if axis == axis_at else 1 for axis in range(len(dims))])
    return loudness


def bell_draw(key, extent, spread, reach, shards=(), kind=jnp.bfloat16):
    drawn = jax.random.normal(key, extent, jnp.float32) * spread
    if len(shards) > 0:
        drawn = block_levels(key, extent, shards, -0.22, 0.18) * drawn
    return jnp.clip(drawn, min=-reach, max=reach).astype(kind)


def setup_inputs(seed: int = 0) -> dict:
    key_list = jax.random.split(jax.random.key(seed), 4)
    return {
        "panel": bell_draw(key_list[0], (ORDER, NB), 0.2, 1.2, ((0, 512),), jnp.float32),
        "inverse_factor": draw_inverse_factor(jax.random.fold_in(key_list[3], 71), 0),
        "slab": bell_draw(key_list[2], (ORDER, SLAB), 1.0, 6.0, ((0, 64), (1, 8))),
    }


def reference(panel, inverse_factor, slab):
    factor_panel = jnp.dot(panel, inverse_factor.T, precision=lax.Precision.HIGHEST, preferred_element_type=jnp.float32).astype(jnp.bfloat16)
    column_index = jnp.arange(SLAB, dtype=jnp.int32)
    owner_col = column_index // SLAB_DEV
    local_col = column_index % SLAB_DEV
    tile_index = (local_col // TILE) * N_COL + owner_col
    matrix_rows = (tile_index * M_DEV + local_col % TILE).astype(jnp.int32)
    mirror = factor_panel[matrix_rows]
    mirror_blocks = mirror.reshape(N_COL, SLAB_DEV, NB)
    slab_blocks = slab.reshape(ORDER, N_COL, SLAB_DEV).transpose(1, 0, 2)

    def update(pair):
        block, rows = pair
        product = jnp.dot(factor_panel, rows.T, preferred_element_type=jnp.float32)
        return (block.astype(jnp.float32) - product).astype(jnp.bfloat16)

    updated = lax.map(update, (slab_blocks, mirror_blocks))
    updated_slab = updated.transpose(1, 0, 2).reshape(ORDER, SLAB)
    return factor_panel, updated_slab
```

```python
import jax
import jax.numpy as jnp
from jax import lax
from jax.sharding import PartitionSpec as P

TILE = 128
ROWS = 64
COLS = 8
PIECE = TILE // COLS
Y = 4
Z = 16
Y_GROUPS = [[z * Y + y for y in range(Y)] for z in range(Z)]
Z_GROUPS = [[z * Y + y for z in range(Z)] for y in range(Y)]
MESH_AXES = ("row", "col")


def device(row, col):
    return row * COLS + col


def permute(value, target):
    return lax.ppermute(
        value,
        MESH_AXES,
        [(device(r, c), device(*target(r, c))) for r in range(ROWS) for c in range(COLS)],
    )


def solve_panel(rows, inverse_factor):
    return lax.dot_general(
        rows,
        inverse_factor,
        (((1,), (1,)), ((), ())),
        precision=lax.Precision.HIGHEST,
        preferred_element_type=jnp.float32,
    ).astype(jnp.bfloat16)


def spread(value, axis, groups, count):
    copies = jnp.broadcast_to(value[None], (count,) + value.shape)
    return lax.all_to_all(copies, axis, 0, 0, axis_index_groups=groups, tiled=True)


def shards(panel, inverse_factor, slab):
    own_factor = solve_panel(panel, inverse_factor)
    pieces = lax.all_to_all(
        own_factor.reshape(COLS, PIECE, -1), "col", 0, 0, tiled=True
    )
    piece = permute(pieces[0], lambda r, c: (r // COLS * COLS + c, r % COLS))
    along_z = spread(piece, "row", Z_GROUPS, Z)
    blocks = [own_factor] + [
        permute(own_factor, lambda r, c, k=k: (r, (c + 2 * k) % COLS)) for k in (1, 2, 3)
    ]
    mine = jnp.stack(blocks)
    other = permute(mine, lambda r, c: (r, c ^ 1))
    my_col = lax.axis_index("col")
    core = my_col % 2
    pair = jnp.where(core == 0, jnp.stack([mine, other], 1), jnp.stack([other, mine], 1))
    x = my_col // 2
    order = (x - jnp.arange(4)) % 4
    factor_rows = pair[order].reshape(COLS * TILE, -1)
    along_y = spread(along_z, "row", Y_GROUPS, Y)
    mirror = along_y.reshape(Y, 8, 2, PIECE, -1).transpose(1, 2, 0, 3, 4).reshape(8 * TILE, -1)
    product = lax.dot_general(
        factor_rows, mirror, (((1,), (1,)), ((), ())), preferred_element_type=jnp.float32
    )
    return own_factor, (slab.astype(jnp.float32) - product).astype(jnp.bfloat16)


def solution(mesh):
    return jax.shard_map(
        shards,
        mesh=mesh,
        in_specs=(P(("row", "col"), None), P(), P("row", "col")),
        out_specs=(P(("row", "col"), None), P("row", "col")),
        check_vma=False,
    )
```

```python
import jax
import jax.numpy as jnp
from jax import lax
from jax.experimental import pallas as pl
from jax.experimental.pallas import tpu as pltpu
from jax.sharding import PartitionSpec as P

NB = 512
TILE = 128
ROWS = 64
COLS = 8
CHIPS = COLS // 2
PIECE = TILE // COLS
BLOCK = ROWS // COLS
WIDE = 2 * TILE
T_ORDER = [6, 7, 0, 1, 2, 3, 4, 5]
J_ORDER = [4, 5, 6, 7, 0, 1, 2, 3]
APART = [[t * COLS + j for t in T_ORDER] for j in range(COLS)]
NEAR = [[t * COLS + j for j in J_ORDER] for t in range(BLOCK)]
MESH_AXES = ("row", "col")


def device(row, col):
    return row * COLS + col


def permute(value, pairs):
    return lax.ppermute(value, MESH_AXES, [(device(*a), device(*b)) for a, b in pairs])


def everywhere(target):
    return [((r, c), target(r, c)) for r in range(ROWS) for c in range(COLS)]


def solve_panel(rows, inverse_factor):
    return lax.dot_general(
        rows,
        inverse_factor,
        (((1,), (1,)), ((), ())),
        precision=lax.Precision.HIGHEST,
        preferred_element_type=jnp.float32,
    ).astype(jnp.bfloat16)


def spread(value, axis, groups, count):
    copies = jnp.broadcast_to(value[None], (count,) + value.shape)
    return lax.all_to_all(copies, axis, 0, 0, axis_index_groups=groups, tiled=True)


def scatter(tile):
    half = COLS // 2 * PIECE
    taken = permute(tile, [((r, 0), (r, 1)) for r in range(ROWS)])
    part = jnp.where(lax.axis_index("col") == 0, tile[:half], taken[half:])
    total = None
    for j in range(COLS // 2):
        pairs = [
            ((t + c, h), (t + h * (COLS // 2) + j, c))
            for t in range(0, ROWS, COLS)
            for c in range(COLS)
            for h in range(2)
        ]
        got = permute(part[j * PIECE : (j + 1) * PIECE], pairs)
        total = got if total is None else total + got
    return total


def assemble(mine, other):
    my_col = lax.axis_index("col")
    chip, core = my_col // 2, my_col % 2
    pair = jnp.where(core == 0, jnp.stack([mine, other], 1), jnp.stack([other, mine], 1))
    pair = pair.reshape(2, 2, WIDE, NB)
    pair = jnp.where(chip % 2 == 0, pair, pair[:, ::-1])
    pair = jnp.where(chip // 2 == 0, pair, pair[::-1])
    return pair.reshape(COLS * TILE, NB)


def shards(panel, inverse_factor, slab):
    own_factor = solve_panel(panel, inverse_factor)
    one = permute(own_factor, everywhere(lambda r, c: (r, c ^ 2)))
    leading = scatter(panel)
    piece = solve_panel(leading, inverse_factor)
    copies = jnp.broadcast_to(piece[None], (BLOCK, PIECE, NB))
    two = jnp.stack([own_factor, one])
    far = lax.all_to_all(copies, "row", 0, 0, axis_index_groups=APART, tiled=True)
    four = jnp.concatenate([two, permute(two, everywhere(lambda r, c: (r, c ^ 4)))])
    far, four = lax.optimization_barrier((far, four))
    near = spread(far, "row", NEAR, COLS)
    other = permute(four, everywhere(lambda r, c: (r, c ^ 1)))
    factor_rows = assemble(four, other)
    near = near.reshape(COLS, BLOCK, PIECE, NB)
    mirror = jnp.concatenate(
        [near[J_ORDER.index(j), T_ORDER.index(t)] for t in range(BLOCK) for j in range(COLS)]
    )
    product = lax.dot_general(
        factor_rows, mirror, (((1,), (1,)), ((), ())), preferred_element_type=jnp.float32
    )
    return own_factor, (slab.astype(jnp.float32) - product).astype(jnp.bfloat16)


def solution(mesh):
    return jax.shard_map(
        shards,
        mesh=mesh,
        in_specs=(P(("row", "col"), None), P(), P("row", "col")),
        out_specs=(P(("row", "col"), None), P("row", "col")),
        check_vma=False,
    )
```

```python
import jax
import jax.numpy as jnp
from jax import lax
from jax.experimental import pallas as pl
from jax.experimental.pallas import tpu as pltpu
from jax.sharding import PartitionSpec as P

NB = 512
TILE = 128
ROWS = 64
COLS = 8
CHIPS = COLS // 2
PIECE = TILE // COLS
BLOCK = ROWS // COLS
WIDE = 2 * TILE
T_ORDER = [6, 2, 0, 4, 7, 3, 1, 5]
J_ORDER = [4, 5, 6, 7, 0, 1, 2, 3]
APART = [[t * COLS + j for t in T_ORDER] for j in range(COLS)]
NEAR = [[t * COLS + j for j in J_ORDER] for t in range(BLOCK)]
MESH_AXES = ("row", "col")


def device(row, col):
    return row * COLS + col


def permute(value, pairs):
    return lax.ppermute(value, MESH_AXES, [(device(*a), device(*b)) for a, b in pairs])


def everywhere(target):
    return [((r, c), target(r, c)) for r in range(ROWS) for c in range(COLS)]


def solve_panel(rows, inverse_factor):
    return lax.dot_general(
        rows,
        inverse_factor,
        (((1,), (1,)), ((), ())),
        precision=lax.Precision.HIGHEST,
        preferred_element_type=jnp.float32,
    ).astype(jnp.bfloat16)


def spread(value, axis, groups, count):
    copies = jnp.broadcast_to(value[None], (count,) + value.shape)
    return lax.all_to_all(copies, axis, 0, 0, axis_index_groups=groups, tiled=True)


def scatter(tile):
    half = COLS // 2 * PIECE
    taken = permute(tile, [((r, 0), (r, 1)) for r in range(ROWS)])
    part = jnp.where(lax.axis_index("col") == 0, tile[:half], taken[half:])
    total = None
    for j in range(COLS // 2):
        pairs = [
            ((t + c, h), (t + h * (COLS // 2) + j, c))
            for t in range(0, ROWS, COLS)
            for c in range(COLS)
            for h in range(2)
        ]
        got = permute(part[j * PIECE : (j + 1) * PIECE], pairs)
        total = got if total is None else total + got
    return total


def update_kernel(mine_ref, other_ref, near_ref, slab_ref, out_ref, rows_ref, old_ref, new_ref, in_sem, out_sem):
    steps, rows, wide = old_ref.shape
    reads = [
        pltpu.make_async_copy(slab_ref.at[:, pl.ds(n * wide, wide)], old_ref.at[n], in_sem.at[n])
        for n in range(steps)
    ]
    for read in reads:
        read.start()
    my_col = lax.axis_index("col")
    chip, core = my_col // 2, my_col % 2
    for m in range(CHIPS):
        base = (chip ^ m) * WIDE
        rows_ref[pl.ds(pl.multiple_of(base + core * TILE, TILE), TILE), :] = mine_ref[m]
        rows_ref[pl.ds(pl.multiple_of(base + (1 - core) * TILE, TILE), TILE), :] = other_ref[m]
    writes = []
    for n in range(steps):
        mirror = jnp.concatenate(
            [
                near_ref[J_ORDER.index(j), T_ORDER.index(n * (wide // TILE) + t)]
                for t in range(wide // TILE)
                for j in range(COLS)
            ],
            axis=0,
        )
        reads[n].wait()
        for part in range(2):
            for step in range(part * rows // 2, (part + 1) * rows // 2, 256):
                here = pl.ds(step, 256)
                product = lax.dot_general(
                    rows_ref[here, :], mirror, (((1,), (1,)), ((), ())), preferred_element_type=jnp.float32
                )
                new_ref[n, here, :] = (old_ref[n, here, :].astype(jnp.float32) - product).astype(jnp.bfloat16)
            half = pl.ds(part * rows // 2, rows // 2)
            write = pltpu.make_async_copy(
                new_ref.at[n, half], out_ref.at[half, pl.ds(n * wide, wide)], out_sem.at[n, part]
            )
            write.start()
            writes.append(write)
    for write in writes:
        write.wait()


def update(mine, other, near, slab):
    rows, columns = slab.shape
    whole = pl.BlockSpec(memory_space=pltpu.VMEM)
    outside = pl.BlockSpec(memory_space=pltpu.HBM)
    steps = columns // WIDE
    return pl.pallas_call(
        update_kernel,
        in_specs=[whole, whole, whole, outside],
        out_specs=outside,
        out_shape=jax.ShapeDtypeStruct(slab.shape, slab.dtype),
        scratch_shapes=[
            pltpu.VMEM((rows, NB), jnp.bfloat16),
            pltpu.VMEM((steps, rows, WIDE), jnp.bfloat16),
            pltpu.VMEM((steps, rows, WIDE), jnp.bfloat16),
            pltpu.SemaphoreType.DMA((steps,)),
            pltpu.SemaphoreType.DMA((steps, 2)),
        ],
        compiler_params=pltpu.CompilerParams(vmem_limit_bytes=51 * 1024 * 1024),
        cost_estimate=pl.CostEstimate(
            flops=2 * rows * columns * NB, bytes_accessed=6 * rows * columns, transcendentals=0
        ),
    )(mine, other, near, slab)


def shards(panel, inverse_factor, slab):
    own_factor = solve_panel(panel, inverse_factor)
    leading = scatter(panel)
    piece = solve_panel(leading, inverse_factor)
    copies = jnp.broadcast_to(piece[None], (BLOCK, PIECE, NB))
    copies, own_rows = lax.optimization_barrier((copies, own_factor))
    far = lax.all_to_all(copies, "row", 0, 0, axis_index_groups=APART, tiled=True)
    one = permute(own_rows, everywhere(lambda r, c: (r, c ^ 2)))
    three = permute(own_rows, everywhere(lambda r, c: (r, c ^ 6)))
    far, one, three, own_late = lax.optimization_barrier((far, one, three, own_rows))
    near = spread(far, "row", NEAR, COLS)
    two = permute(own_late, everywhere(lambda r, c: (r, c ^ 4)))
    four = jnp.stack([own_late, one, two, three])
    other = permute(four, everywhere(lambda r, c: (r, c ^ 1)))
    updated_slab = update(four, other, near.reshape(COLS, BLOCK, PIECE, NB), slab)
    return own_factor, updated_slab


def solution(mesh):
    return jax.shard_map(
        shards,
        mesh=mesh,
        in_specs=(P(("row", "col"), None), P(), P("row", "col")),
        out_specs=(P(("row", "col"), None), P("row", "col")),
        check_vma=False,
    )
```

```python
import jax
import jax.numpy as jnp
from jax import lax
from jax.experimental import pallas as pl
from jax.experimental.pallas import tpu as pltpu
from jax.sharding import PartitionSpec as P

NB = 512
TILE = 128
ROWS = 64
COLS = 8
CHIPS = COLS // 2
PIECE = TILE // COLS
BLOCK = ROWS // COLS
WIDE = 2 * TILE
T_ORDER = [6, 2, 0, 4, 7, 3, 1, 5]
J_ORDER = [4, 5, 6, 7, 0, 1, 2, 3]
APART = [[t * COLS + j for t in T_ORDER] for j in range(COLS)]
NEAR = [[t * COLS + j for j in J_ORDER] for t in range(BLOCK)]
MESH_AXES = ("row", "col")


def device(row, col):
    return row * COLS + col


def permute(value, pairs):
    return lax.ppermute(value, MESH_AXES, [(device(*a), device(*b)) for a, b in pairs])


def everywhere(target):
    return [((r, c), target(r, c)) for r in range(ROWS) for c in range(COLS)]


def solve_panel(rows, inverse_factor):
    return lax.dot_general(
        rows,
        inverse_factor,
        (((1,), (1,)), ((), ())),
        precision=lax.Precision.HIGHEST,
        preferred_element_type=jnp.float32,
    ).astype(jnp.bfloat16)


def spread(value, axis, groups, count):
    copies = jnp.broadcast_to(value[None], (count,) + value.shape)
    return lax.all_to_all(copies, axis, 0, 0, axis_index_groups=groups, tiled=True)


def scatter(tile):
    half = COLS // 2 * PIECE
    taken = permute(tile, [((r, 0), (r, 1)) for r in range(ROWS)])
    part = jnp.where(lax.axis_index("col") == 0, tile[:half], taken[half:])
    total = None
    for j in range(COLS // 2):
        pairs = [
            ((t + c, h), (t + h * (COLS // 2) + j, c))
            for t in range(0, ROWS, COLS)
            for c in range(COLS)
            for h in range(2)
        ]
        got = permute(part[j * PIECE : (j + 1) * PIECE], pairs)
        total = got if total is None else total + got
    return total


def update_kernel(mine_ref, other_ref, near_ref, slab_ref, out_ref, rows_ref, old_ref, new_ref, in_sem, out_sem):
    steps, rows, wide = old_ref.shape
    reads = [
        pltpu.make_async_copy(slab_ref.at[:, pl.ds(n * wide, wide)], old_ref.at[n], in_sem.at[n])
        for n in range(steps)
    ]
    for read in reads:
        read.start()
    my_col = lax.axis_index("col")
    chip, core = my_col // 2, my_col % 2
    for m in range(CHIPS):
        base = (chip ^ m) * WIDE
        rows_ref[pl.ds(pl.multiple_of(base + core * TILE, TILE), TILE), :] = mine_ref[m]
        rows_ref[pl.ds(pl.multiple_of(base + (1 - core) * TILE, TILE), TILE), :] = other_ref[m]
    writes = []
    for n in range(steps):
        mirror = jnp.concatenate(
            [
                near_ref[J_ORDER.index(j), T_ORDER.index(n * (wide // TILE) + t)]
                for t in range(wide // TILE)
                for j in range(COLS)
            ],
            axis=0,
        )
        reads[n].wait()
        for part in range(2):
            for step in range(part * rows // 2, (part + 1) * rows // 2, 256):
                here = pl.ds(step, 256)
                product = lax.dot_general(
                    rows_ref[here, :], mirror, (((1,), (1,)), ((), ())), preferred_element_type=jnp.float32
                )
                new_ref[n, here, :] = (old_ref[n, here, :].astype(jnp.float32) - product).astype(jnp.bfloat16)
            half = pl.ds(part * rows // 2, rows // 2)
            write = pltpu.make_async_copy(
                new_ref.at[n, half], out_ref.at[half, pl.ds(n * wide, wide)], out_sem.at[n, part]
            )
            write.start()
            writes.append(write)
    for write in writes:
        write.wait()


def update(mine, other, near, slab):
    rows, columns = slab.shape
    whole = pl.BlockSpec(memory_space=pltpu.VMEM)
    outside = pl.BlockSpec(memory_space=pltpu.HBM)
    steps = columns // (2 * WIDE)
    return pl.pallas_call(
        update_kernel,
        in_specs=[whole, whole, whole, outside],
        out_specs=outside,
        out_shape=jax.ShapeDtypeStruct(slab.shape, slab.dtype),
        scratch_shapes=[
            pltpu.VMEM((rows, NB), jnp.bfloat16),
            pltpu.VMEM((steps, rows, 2 * WIDE), jnp.bfloat16),
            pltpu.VMEM((steps, rows, 2 * WIDE), jnp.bfloat16),
            pltpu.SemaphoreType.DMA((steps,)),
            pltpu.SemaphoreType.DMA((steps, 2)),
        ],
        compiler_params=pltpu.CompilerParams(vmem_limit_bytes=51 * 1024 * 1024),
        cost_estimate=pl.CostEstimate(
            flops=2 * rows * columns * NB, bytes_accessed=6 * rows * columns, transcendentals=0
        ),
    )(mine, other, near, slab)


def shards(panel, inverse_factor, slab):
    own_factor = solve_panel(panel, inverse_factor)
    leading = scatter(panel)
    piece = solve_panel(leading, inverse_factor)
    copies = jnp.broadcast_to(piece[None], (BLOCK, PIECE, NB))
    copies, own_rows = lax.optimization_barrier((copies, own_factor))
    far = lax.all_to_all(copies, "row", 0, 0, axis_index_groups=APART, tiled=True)
    one = permute(own_rows, everywhere(lambda r, c: (r, c ^ 2)))
    two = permute(own_rows, everywhere(lambda r, c: (r, c ^ 4)))
    far, one, two, own_late = lax.optimization_barrier((far, one, two, own_rows))
    near = spread(far, "row", NEAR, COLS)
    three = permute(own_late, everywhere(lambda r, c: (r, c ^ 6)))
    four = jnp.stack([own_late, one, two, three])
    other = permute(four, everywhere(lambda r, c: (r, c ^ 1)))
    updated_slab = update(four, other, near.reshape(COLS, BLOCK, PIECE, NB), slab)
    return own_factor, updated_slab


def solution(mesh):
    return jax.shard_map(
        shards,
        mesh=mesh,
        in_specs=(P(("row", "col"), None), P(), P("row", "col")),
        out_specs=(P(("row", "col"), None), P("row", "col")),
        check_vma=False,
    )
```

```python
import jax
import jax.numpy as jnp
from jax import lax
from jax.experimental import pallas as pl
from jax.experimental.pallas import tpu as pltpu
from jax.sharding import PartitionSpec as P

NB = 512
TILE = 128
ROWS = 64
COLS = 8
CHIPS = COLS // 2
PIECE = TILE // COLS
BLOCK = ROWS // COLS
WIDE = 2 * TILE
T_ORDER = [6, 2, 0, 4, 7, 3, 1, 5]
J_ORDER = [4, 5, 6, 7, 0, 1, 2, 3]
APART = [[t * COLS + j for t in T_ORDER] for j in range(COLS)]
NEAR = [[t * COLS + j for j in J_ORDER] for t in range(BLOCK)]
MESH_AXES = ("row", "col")


def device(row, col):
    return row * COLS + col


def permute(value, pairs):
    return lax.ppermute(value, MESH_AXES, [(device(*a), device(*b)) for a, b in pairs])


def everywhere(target):
    return [((r, c), target(r, c)) for r in range(ROWS) for c in range(COLS)]


def solve_panel(rows, inverse_factor):
    return lax.dot_general(
        rows,
        inverse_factor,
        (((1,), (1,)), ((), ())),
        precision=lax.Precision.HIGHEST,
        preferred_element_type=jnp.float32,
    ).astype(jnp.bfloat16)


def spread(value, axis, groups, count):
    copies = jnp.broadcast_to(value[None], (count,) + value.shape)
    return lax.all_to_all(copies, axis, 0, 0, axis_index_groups=groups, tiled=True)


def scatter(tile):
    half = COLS // 2 * PIECE
    taken = permute(tile, [((r, 0), (r, 1)) for r in range(ROWS)])
    part = jnp.where(lax.axis_index("col") == 0, tile[:half], taken[half:])
    total = None
    for j in range(COLS // 2):
        pairs = [
            ((t + c, h), (t + h * (COLS // 2) + j, c))
            for t in range(0, ROWS, COLS)
            for c in range(COLS)
            for h in range(2)
        ]
        got = permute(part[j * PIECE : (j + 1) * PIECE], pairs)
        total = got if total is None else total + got
    return total


def update_kernel(mine_ref, other_ref, near_ref, slab_ref, out_ref, rows_ref, old_ref, new_ref, in_sem, out_sem):
    steps, rows, wide = old_ref.shape
    reads = [
        pltpu.make_async_copy(slab_ref.at[:, pl.ds(n * wide, wide)], old_ref.at[n], in_sem.at[n])
        for n in range(steps)
    ]
    for read in reads:
        read.start()
    my_col = lax.axis_index("col")
    chip, core = my_col // 2, my_col % 2
    for m in range(CHIPS):
        base = (chip ^ m) * WIDE
        rows_ref[pl.ds(pl.multiple_of(base + core * TILE, TILE), TILE), :] = mine_ref[m]
        rows_ref[pl.ds(pl.multiple_of(base + (1 - core) * TILE, TILE), TILE), :] = other_ref[m]
    writes = []
    for n in range(steps):
        mirror = jnp.concatenate(
            [
                near_ref[J_ORDER.index(j), T_ORDER.index(n * (wide // TILE) + t)]
                for t in range(wide // TILE)
                for j in range(COLS)
            ],
            axis=0,
        )
        reads[n].wait()
        for part in range(2):
            for step in range(part * rows // 2, (part + 1) * rows // 2, 256):
                here = pl.ds(step, 256)
                product = lax.dot_general(
                    rows_ref[here, :], mirror, (((1,), (1,)), ((), ())), preferred_element_type=jnp.float32
                )
                new_ref[n, here, :] = (old_ref[n, here, :].astype(jnp.float32) - product).astype(jnp.bfloat16)
            half = pl.ds(part * rows // 2, rows // 2)
            write = pltpu.make_async_copy(
                new_ref.at[n, half], out_ref.at[half, pl.ds(n * wide, wide)], out_sem.at[n, part]
            )
            write.start()
            writes.append(write)
    for write in writes:
        write.wait()


def update(mine, other, near, slab):
    rows, columns = slab.shape
    whole = pl.BlockSpec(memory_space=pltpu.VMEM)
    outside = pl.BlockSpec(memory_space=pltpu.HBM)
    steps = columns // (2 * WIDE)
    return pl.pallas_call(
        update_kernel,
        in_specs=[whole, whole, whole, outside],
        out_specs=outside,
        out_shape=jax.ShapeDtypeStruct(slab.shape, slab.dtype),
        scratch_shapes=[
            pltpu.VMEM((rows, NB), jnp.bfloat16),
            pltpu.VMEM((steps, rows, 2 * WIDE), jnp.bfloat16),
            pltpu.VMEM((steps, rows, 2 * WIDE), jnp.bfloat16),
            pltpu.SemaphoreType.DMA((steps,)),
            pltpu.SemaphoreType.DMA((steps, 2)),
        ],
        compiler_params=pltpu.CompilerParams(vmem_limit_bytes=51 * 1024 * 1024),
        cost_estimate=pl.CostEstimate(
            flops=2 * rows * columns * NB, bytes_accessed=6 * rows * columns, transcendentals=0
        ),
    )(mine, other, near, slab)


def shards(panel, inverse_factor, slab):
    leading = scatter(panel)
    piece = solve_panel(leading, inverse_factor)
    copies = jnp.broadcast_to(piece[None], (BLOCK, PIECE, NB))
    copies, late_panel = lax.optimization_barrier((copies, panel))
    own_factor = solve_panel(late_panel, inverse_factor)
    own_rows = own_factor
    far = lax.all_to_all(copies, "row", 0, 0, axis_index_groups=APART, tiled=True)
    one = permute(own_rows, everywhere(lambda r, c: (r, c ^ 2)))
    two = permute(own_rows, everywhere(lambda r, c: (r, c ^ 4)))
    far, one, two, own_late = lax.optimization_barrier((far, one, two, own_rows))
    near = spread(far, "row", NEAR, COLS)
    three = permute(own_late, everywhere(lambda r, c: (r, c ^ 6)))
    four = jnp.stack([own_late, one, two, three])
    other = permute(four, everywhere(lambda r, c: (r, c ^ 1)))
    updated_slab = update(four, other, near.reshape(COLS, BLOCK, PIECE, NB), slab)
    return own_factor, updated_slab


def solution(mesh):
    return jax.shard_map(
        shards,
        mesh=mesh,
        in_specs=(P(("row", "col"), None), P(), P("row", "col")),
        out_specs=(P(("row", "col"), None), P("row", "col")),
        check_vma=False,
    )
```
